256 devices in a mesh: row: 8 (over z_hi, core), col: 32 (over z_lo, x, y).
Axes of the slice: x: 4, y: 4, z: 8 (z_hi: 4, z_lo: 2; z = z_hi * 2 + z_lo), core: 2. Of those that a mesh axis runs over, the one named last changes fastest.
Arguments:
- inputs: float32 [1024, 6144], P('col', 'row'), may hold values from -6 to 6
- in_weight: float32 [6144, 24576], P('row', 'col'), may hold values from -0.078125 to 0.078125
- in_bias: float32 [24576], P('col'), may hold values from -3 to 3
- out_weight: float32 [24576, 6144], P('col', 'row'), may hold values from -0.0390625 to 0.0390625
- out_grad: float32 [1024, 6144], P('col', 'row'), may hold values from -0.875 to 0.875
Outputs:
- outputs: float32 [1024, 6144], P('col', 'row')
- grad_in: float32 [1024, 6144], P('col', 'row')
- grad_w_in: float32 [6144, 24576], P('row', 'col')
- grad_bias: float32 [24576], P('col')
- grad_w_out: float32 [24576, 6144], P('col', 'row')
The draws below stay inside these ranges and needn't reach their ends.
All inputs are finite; a program needn't handle non-finite values.
Results may differ from the reference program's by a relative error of at most 0.00011.
Values sent between devices are 32-bit elements; how exact they have to be, the bound alone decides.
A program may use at most 128 MiB of HBM per device.

```python
import jax
import jax.numpy as jnp
from jax import lax

D = 6144
FF = 24576
TOKENS = 1024


def shard_levels(own_key, extent, pieces, least, top_value):
    gain = 1.0
    for position, blocks in pieces:
        heights = jax.random.uniform(jax.random.fold_in(jax.random.fold_in(own_key, 6), position), (blocks,), jnp.float32, least / len(pieces), top_value / len(pieces))
        gain = gain * jnp.repeat(jnp.exp(heights), extent[position] // blocks).reshape((-1,) + (1,) * (len(extent) - 1 - position))
    return gain


def centred(key, dims, deviation, bound, split=(), held_as=jnp.bfloat16):
    loudness = shard_levels(key, dims, split, -0.22, 0.18) if split else 1.0
    drawn = jax.random.normal(key, dims, jnp.float32) * deviation * loudness
    return jnp.minimum(jnp.maximum(drawn, -bound), bound).astype(held_as)


def setup_inputs(seed: int = 0) -> dict:
    streams_of = jax.random.split(jax.random.key(seed), 6)
    return {
        "inputs": centred(streams_of[0], (TOKENS, D), 1.0, 6.0, ((0, 32), (1, 8)), jnp.float32),
        "in_weight": centred(streams_of[1], (D, FF), D ** -0.5, 0.078125, ((0, 8), (1, 32)), jnp.float32),
        "in_bias": centred(streams_of[2], (FF,), 0.5, 3.0, ((0, 32),), jnp.float32),
        "out_weight": centred(streams_of[3], (FF, D), FF ** -0.5, 0.0390625, ((0, 32), (1, 8)), jnp.float32),
        "out_grad": centred(streams_of[4], (TOKENS, D), 0.15, 0.875, ((0, 32), (1, 8)), jnp.float32),
    }


inv_root_two = 0.7071067811865476
inv_root_two_pi = 0.3989422804014327


def matmul_high(left, right):
    return jnp.dot(left, right, precision=lax.Precision.HIGHEST, preferred_element_type=jnp.float32)


def gelu_parts(pre):
    cdf = 0.5 * (1.0 + lax.erf(pre * inv_root_two))
    activated = pre * cdf
    slopes = cdf + pre * jnp.exp(-0.5 * pre * pre) * inv_root_two_pi
    return activated, slopes


def reference(inputs, in_weight, in_bias, out_weight, out_grad):
    pre = matmul_high(inputs, in_weight) + in_bias
    activated, slopes = gelu_parts(pre)
    outputs = matmul_high(activated, out_weight)
    grad_w_out = matmul_high(activated.T, out_grad)
    grad_pre = matmul_high(out_grad, out_weight.T) * slopes
    grad_bias = jnp.sum(grad_pre, axis=0)
    grad_w_in = matmul_high(inputs.T, grad_pre)
    grad_in = matmul_high(grad_pre, in_weight.T)
    return outputs, grad_in, grad_w_in, grad_bias, grad_w_out
```

```python
import jax
import jax.numpy as jnp
from jax import lax
from jax.experimental import pallas as pl
from jax.experimental.pallas import tpu as pltpu
from jax.sharding import PartitionSpec as P

MESH = pl.DeviceIdType.MESH
F32 = jnp.float32
BF16 = jnp.bfloat16

inv_root_two = 0.7071067811865476
inv_root_two_pi = 0.3989422804014327

UNITS = ((0, (0, 1)), (1, (0, 1)), (2, (0, 1)), (3, (0, 1)))
SCHEDULE = (
    "A0 0", "A0 1", "A0 2", "A0 3", "A1 0", "W 0", "A2 0", "A1 1", "W 1",
    "B 0", "C 0", "A2 1", "A1 2", "D 0", "B 1", "C 1", "A2 2", "A1 3", "E 0",
    "D 1", "B 2", "C 2", "A2 3", "F 0", "E 1", "D 2", "B 3", "C 3", "G 0", "M 0",
    "F 1", "E 2", "D 3", "N 0", "R 0", "G 1", "M 1", "F 2", "E 3", "S 0", "N 1", "R 1",
    "G 2", "M 2", "F 3", "S 1", "T 0", "N 2", "R 2", "G 3", "M 3", "S 2", "T 1", "R 3", "N 3",
    "S 3", "T 2", "T 3",
)
WIDTH = 768
TILE = 256


def split(value):
    high = value.astype(BF16)
    return high, (value - high.astype(F32)).astype(BF16)


def dot(left, right):
    return lax.dot_general(left, right, (((1,), (0,)), ((), ())), preferred_element_type=F32)


def dot3(left, left_at, right, right_at, columns):
    high, low = left[left_at, 0], left[left_at, 1]
    right_high, right_low = right[right_at, 0, :, columns], right[right_at, 1, :, columns]
    return dot(high, right_high) + (dot(high, right_low) + dot(low, right_high))


def tiles(body):
    @pl.loop(0, WIDTH // TILE)
    def _(step):
        body(pl.ds(pl.multiple_of(step * TILE, TILE), TILE))


def kernel(
    inputs, in_weight, in_bias, out_weight, out_grad,
    outputs, grad_in, grad_w_in, grad_bias, grad_w_out,
    wide, weights, left, turned, right, bias, bias_sum, results,
    local_sem, send_sem, recv_sem, *buffers,
):
    row, col = lax.axis_index("row"), lax.axis_index("col")
    zh, core = lax.div(row, 2), lax.rem(row, 2)
    zl, x, y = lax.div(col, 16), lax.rem(lax.div(col, 4), 4), lax.rem(col, 4)

    def device(dz=0, dc=0, dl=0, dx=0, dy=0):
        return (
            lax.rem(zh + dz, 4) * 2 + lax.rem(core + dc, 2),
            lax.rem(zl + dl, 2) * 16 + lax.rem(x + dx, 4) * 4 + lax.rem(y + dy, 4),
        )

    units = [tuple(buffers[8 * u : 8 * u + 8]) for u in range(len(UNITS))]
    count = [0, 0]
    sent = []
    waiting = {}

    def local(src, dst):
        copy = pltpu.make_async_copy(src, dst, local_sem.at[count[0]])
        count[0] += 1
        copy.start()
        return copy

    def send(key, src, dst, to):
        copy = pltpu.make_async_remote_copy(
            src, dst, send_sem.at[count[1]], recv_sem.at[count[1]], device_id=to, device_id_type=MESH
        )
        count[1] += 1
        copy.start()
        waiting[key] = copy
        sent.append(copy)

    def arrived(*key):
        waiting[key].wait_recv()

    barrier = pltpu.get_barrier_semaphore()
    partners = [
        device(dz=1), device(dz=3), device(dc=1), device(dl=1),
        device(dx=1), device(dx=2), device(dx=3), device(dy=1), device(dy=2), device(dy=3),
    ]
    for partner in partners:
        pl.semaphore_signal(barrier, 1, device_id=partner, device_id_type=MESH)

    weight_copies = [local(in_weight, wide.at[0]), local(out_weight, wide.at[1])]
    bias_copy = local(in_bias, bias)
    own_copies = {}
    for u, (block, planes) in enumerate(UNITS):
        gathered = units[u][0]
        for a, source in enumerate((inputs, out_grad)):
            own_copies[u, a] = local(source.at[block], gathered.at[a, y, x, zl])
    pl.semaphore_wait(barrier, len(partners))

    def shard(ref, lead, owner_core, owner):
        return ref.at[(*lead, owner_core * 2 + lax.div(owner, 2), pl.ds(lax.rem(owner, 2) * 2, 2))]

    def half(ref, lead, owner_core):
        return ref.at[(*lead, pl.ds(owner_core * 2, 2))]

    def part(ref, lead, owner):
        return ref.at[(*lead, lax.div(owner, 2), pl.ds(lax.rem(owner, 2) * 2, 2))]

    up, down = lax.rem(zh + 1, 4), lax.rem(zh + 3, 4)
    far = lax.rem(zh + 2, 4)

    def a0(u):
        gathered = units[u][0]
        for a, source in enumerate((inputs, out_grad)):
            send((u, "a0", a), source.at[UNITS[u][0]], gathered.at[a, y, x, zl], device(dl=1))

    def a1(u):
        gathered = units[u][0]
        for a in range(2):
            own_copies[u, a].wait()
            arrived(u, "a0", a)
            for o in range(1, 4):
                to = device(dx=o) if a == 0 else device(dy=o)
                block = gathered.at[a, y, x]
                send((u, "a1", a, o), block, block, to)

    def a2(u):
        gathered = units[u][0]
        for a in range(2):
            for o in range(1, 4):
                arrived(u, "a1", a, o)
            for o in range(1, 4):
                to = device(dy=o) if a == 0 else device(dx=o)
                block = gathered.at[0, y] if a == 0 else gathered.at[1, :, x]
                send((u, "a2", a, o), block, block, to)

    def prepare(which):
        weight_copies[which].wait()

        def body(columns):
            high, low = split(wide[which, :, columns])
            weights[which, 0, :, columns] = high
            weights[which, 1, :, columns] = low
            high, low = split(wide[which, :, columns].T)
            weights[2 + which, 0, columns, :] = high
            weights[2 + which, 1, columns, :] = low

        tiles(body)

    def flat(value):
        return value.reshape(-1, WIDTH)

    def project(u):
        gathered, partial, from_core = units[u][0], units[u][1], units[u][2]
        shape = partial.shape[1:-1]
        rows = shape[0] * shape[1] * shape[2] * shape[3]
        for a in range(2):
            for o in range(1, 4):
                arrived(u, "a2", a, o)
            high, low = split(flat(gathered[a]))
            left[0, 0, :rows] = high
            left[0, 1, :rows] = low

            def body(columns, a=a):
                value = dot3(left, 0, weights, 0 if a == 0 else 3, columns)
                partial[a, :, :, :, :, columns] = value.reshape(*shape, TILE)

            tiles(body)
            send((u, "b", a), half(partial, (a,), 1 - core), from_core.at[a], device(dc=1))

    def reduce_start(u):
        partial, from_core, ring = units[u][1], units[u][2], units[u][3]
        for a in range(2):
            arrived(u, "b", a)
            from_core[a] = from_core[a] + half(partial, (a,), core)[...]
        send((u, "c", 0), part(from_core, (0,), far), ring.at[0], device(dz=1))
        send((u, "c", 1), part(from_core, (1,), far), ring.at[1], device(dz=3))
        send((u, "c", 2), part(from_core, (1,), up), ring.at[2], device(dz=1))
        send((u, "c", 3), part(from_core, (0,), down), ring.at[3], device(dz=3))

    def reduce_relay(u):
        from_core, ring = units[u][2], units[u][3]
        arrived(u, "c", 0)
        ring[0] = ring[0] + part(from_core, (0,), up)[...]
        send((u, "d", 0), ring.at[0], ring.at[4], device(dz=1))
        arrived(u, "c", 1)
        ring[1] = ring[1] + part(from_core, (1,), down)[...]
        send((u, "d", 1), ring.at[1], ring.at[5], device(dz=3))

    def activate(u):
        from_core, ring, hidden = units[u][2], units[u][3], units[u][4]
        arrived(u, "c", 2)
        arrived(u, "c", 3)
        arrived(u, "d", 0)
        arrived(u, "d", 1)
        pre = flat(part(from_core, (0,), zh)[...] + (ring[3] + ring[4])) + bias[...]
        grad_act = flat(part(from_core, (1,), zh)[...] + (ring[2] + ring[5]))
        cdf = 0.5 * (1.0 + lax.erf(pre * inv_root_two))
        slopes = cdf + pre * jnp.exp(-0.5 * pre * pre) * inv_root_two_pi
        shape = ring.shape[1:]
        shard(hidden, (0,), core, zh)[...] = (pre * cdf).reshape(shape)
        shard(hidden, (1,), core, zh)[...] = (grad_act * slopes).reshape(shape)
        block = shard(hidden, (slice(None),), core, zh)
        send((u, "e", 0), block, block, device(dz=1))
        send((u, "e", 1), block, block, device(dz=3))
        send((u, "e", 2), block, block, device(dc=1))

    def gather_relay(u):
        hidden = units[u][4]
        arrived(u, "e", 0)
        block = shard(hidden, (0,), core, down)
        send((u, "f", 0), block, block, device(dz=1))
        arrived(u, "e", 1)
        block = shard(hidden, (1,), core, up)
        send((u, "f", 1), block, block, device(dz=3))
        block = shard(hidden, (slice(None),), core, down)
        send((u, "f", 2), block, block, device(dc=1))
        block = shard(hidden, (slice(None),), core, up)
        send((u, "f", 3), block, block, device(dc=1))

    def gather_last(u):
        hidden = units[u][4]
        for a in range(2):
            arrived(u, "f", a)
            block = shard(hidden, (a,), core, far)
            send((u, "g", a), block, block, device(dc=1))

    def expand(u):
        partial, hidden, first = units[u][1], units[u][4], units[u][5]
        shape = partial.shape[1:-1]
        rows = shape[0] * shape[1] * shape[2] * shape[3]
        arrived(u, "e", 2)
        arrived(u, "f", 2)
        arrived(u, "f", 3)
        arrived(u, "g", 0)
        arrived(u, "g", 1)
        for a in range(2):
            high, low = split(flat(hidden[a]))
            left[a, 0, :rows] = high
            left[a, 1, :rows] = low
            waiting[u, "b", a].wait_send()

            def body(columns, a=a):
                value = dot3(left, a, weights, 1 if a == 0 else 2, columns)
                partial[a, :, :, :, :, columns] = value.reshape(*shape, TILE)

            tiles(body)
            for o in range(1, 4):
                if a == 0:
                    block, to = partial.at[0, lax.rem(y + o, 4)], device(dy=o)
                else:
                    block, to = partial.at[1, :, lax.rem(x + o, 4)], device(dx=o)
                send((u, "r", a, o), block, first.at[a, o - 1], to)

    def weight_grads(u):
        gathered, hidden = units[u][0], units[u][4]
        rows = gathered.shape[1] * gathered.shape[2] * gathered.shape[3] * gathered.shape[4]
        high, low = split(flat(hidden[0]).T)
        turned[0, 0, :, :rows] = high
        turned[0, 1, :, :rows] = low
        high, low = split(flat(gathered[0]).T)
        turned[1, 0, :, :rows] = high
        turned[1, 1, :, :rows] = low
        high, low = split(flat(gathered[1]))
        right[0, :rows] = high
        right[1, :rows] = low
        total = jnp.sum(flat(hidden[1]), axis=0, keepdims=True)
        bias_sum[...] = total if u == 0 else bias_sum[...] + total

        def body(columns):
            for which in range(2):
                high, low = turned[which, 0, :, :rows], turned[which, 1, :, :rows]
                if which == 0:
                    right_high, right_low = right[0, :rows, columns], right[1, :rows, columns]
                else:
                    right_high, right_low = left[1, 0, :rows, columns], left[1, 1, :rows, columns]
                value = dot(high, right_high) + (dot(high, right_low) + dot(low, right_high))
                wide[which, :, columns] = value if u == 0 else wide[which, :, columns] + value

        tiles(body)

    def scatter_first(u):
        partial, first, second = units[u][1], units[u][5], units[u][6]
        for a in range(2):
            for o in range(1, 4):
                arrived(u, "r", a, o)
            own = partial[0, y] if a == 0 else partial[1, :, x]
            first[a, 0] = own + first[a, 0] + (first[a, 1] + first[a, 2])
            for o in range(1, 4):
                if a == 0:
                    block, to = first.at[0, 0, lax.rem(x + o, 4)], device(dx=o)
                else:
                    block, to = first.at[1, 0, lax.rem(y + o, 4)], device(dy=o)
                send((u, "s", a, o), block, second.at[a, o - 1], to)

    def scatter_second(u):
        first, second, third = units[u][5], units[u][6], units[u][7]
        for a in range(2):
            for o in range(1, 4):
                arrived(u, "s", a, o)
            own = first[0, 0, x] if a == 0 else first[1, 0, y]
            second[a, 0] = own + second[a, 0] + (second[a, 1] + second[a, 2])
            send((u, "t", a), second.at[a, 0, 1 - zl], third.at[a], device(dl=1))

    def scatter_last(u):
        second, third = units[u][6], units[u][7]
        block = UNITS[u][0]
        for a in range(2):
            arrived(u, "t", a)
            results[a, block] = second[a, 0, zl] + third[a]

    stages = {
        "A0": a0, "A1": a1, "A2": a2, "W": prepare, "B": project, "C": reduce_start, "D": reduce_relay,
        "E": activate, "F": gather_relay, "G": gather_last, "M": expand, "N": weight_grads,
        "R": scatter_first, "S": scatter_second, "T": scatter_last,
    }
    for entry in SCHEDULE:
        name, u = entry.split()
        if name == "C" and u == "0":
            bias_copy.wait()
        stages[name](int(u))

    finals = [
        local(wide.at[1], grad_w_in), local(wide.at[0], grad_w_out), local(bias_sum, grad_bias),
        local(results.at[0], outputs), local(results.at[1], grad_in),
    ]
    done = {id(waiting[u, "b", a]) for u in range(len(UNITS)) for a in range(2)}
    for copy in sent:
        if id(copy) not in done:
            copy.wait_send()
    for copy in finals:
        copy.wait()


def on_device(inputs, in_weight, in_bias, out_weight, out_grad):
    blocks = inputs.shape[0] // 8
    cut = (blocks, 8, WIDTH)
    buffers = []
    for _, planes in UNITS:
        n = len(planes)
        buffers += [
            pltpu.VMEM((2, 4, 4, n, 8, WIDTH), F32),
            pltpu.VMEM((2, 4, 4, n, 8, WIDTH), F32),
            pltpu.VMEM((2, 2, 4, n, 8, WIDTH), F32),
            pltpu.VMEM((6, 2, n, 8, WIDTH), F32),
            pltpu.VMEM((2, 4, 4, n, 8, WIDTH), F32),
            pltpu.VMEM((2, 3, 4, n, 8, WIDTH), F32),
            pltpu.VMEM((2, 3, n, 8, WIDTH), F32),
            pltpu.VMEM((2, 8, WIDTH), F32),
        ]
    copies = 45 * len(UNITS)
    anywhere = pl.BlockSpec(memory_space=pl.ANY)
    outputs, grad_in, grad_w_in, grad_bias, grad_w_out = pl.pallas_call(
        kernel,
        out_shape=(
            jax.ShapeDtypeStruct(cut, F32),
            jax.ShapeDtypeStruct(cut, F32),
            jax.ShapeDtypeStruct((WIDTH, WIDTH), F32),
            jax.ShapeDtypeStruct((1, WIDTH), F32),
            jax.ShapeDtypeStruct((WIDTH, WIDTH), F32),
        ),
        in_specs=[anywhere] * 5,
        out_specs=[anywhere] * 5,
        scratch_shapes=[
            pltpu.VMEM((2, WIDTH, WIDTH), F32),
            pltpu.VMEM((4, 2, WIDTH, WIDTH), BF16),
            pltpu.VMEM((2, 2, 256, WIDTH), BF16),
            pltpu.VMEM((2, 2, WIDTH, 256), BF16),
            pltpu.VMEM((2, 256, WIDTH), BF16),
            pltpu.VMEM((1, WIDTH), F32),
            pltpu.VMEM((1, WIDTH), F32),
            pltpu.VMEM((2, blocks, 8, WIDTH), F32),
            pltpu.SemaphoreType.DMA((16,)),
            pltpu.SemaphoreType.DMA((copies,)),
            pltpu.SemaphoreType.DMA((copies,)),
            *buffers,
        ],
        compiler_params=pltpu.CompilerParams(
            collective_id=0, has_side_effects=True, vmem_limit_bytes=60 * 2**20
        ),
        name="mlp",
    )(
        inputs.reshape(cut), in_weight, in_bias.reshape(1, WIDTH), out_weight, out_grad.reshape(cut)
    )
    flat = (blocks * 8, WIDTH)
    return outputs.reshape(flat), grad_in.reshape(flat), grad_w_in, grad_bias.reshape(WIDTH), grad_w_out


def solution(mesh):
    in_specs = (P("col", "row"), P("row", "col"), P("col"), P("col", "row"), P("col", "row"))
    out_specs = (P("col", "row"), P("col", "row"), P("row", "col"), P("col"), P("col", "row"))
    return jax.shard_map(
        on_device, mesh=mesh, in_specs=in_specs, out_specs=out_specs, check_vma=False
    )
```

```python
import jax
import jax.numpy as jnp
from jax import lax
from jax.experimental import pallas as pl
from jax.experimental.pallas import tpu as pltpu
from jax.sharding import PartitionSpec as P

MESH = pl.DeviceIdType.MESH
F32 = jnp.float32
BF16 = jnp.bfloat16

inv_root_two = 0.7071067811865476
inv_root_two_pi = 0.3989422804014327

UNITS = ((0, (0,)), (0, (1,)), (1, (0, 1)), (2, (0, 1)), (3, (0,)), (3, (1,)))
SCHEDULE = (
    "A0 1", "W 1", "A0 0", "A1 1", "A1 0", "A0 2", "A2 1", "W 0", "A2 0", "A0 4", "B 1", "A0 3",
    "C 1", "A1 3", "B 0", "A1 2", "A1 4", "C 0", "A2 2", "A0 5", "D 1", "D 0", "E 1", "E 0",
    "B 2", "A2 3", "F 1", "C 2", "A1 5", "D 2", "B 3", "F 0", "C 3", "A2 4", "G 1", "G 0",
    "E 2", "A2 5", "M 0", "B 5", "D 3", "F 2", "E 3", "B 4", "G 2", "M 1", "C 4", "M 2",
    "R 0", "D 4", "F 3", "N 0", "N 1", "C 5", "E 4", "R 1", "R 2", "G 3", "S 1", "M 3",
    "S 2", "D 5", "T 2", "T 1", "S 0", "F 4", "E 5", "G 4", "T 0", "M 4", "F 5", "N 2",
    "G 5", "R 3", "R 4", "M 5", "S 3", "N 3", "R 5", "S 4", "N 4", "S 5", "T 4", "N 5",
    "T 3", "T 5",
)
WIDTH = 768
TILE = 256


def split(value):
    high = value.astype(BF16)
    return high, (value - high.astype(F32)).astype(BF16)


def dot(left, right):
    return lax.dot_general(left, right, (((1,), (0,)), ((), ())), preferred_element_type=F32)


def dot3(left, left_at, rows, right, right_at, columns):
    high, low = left[left_at, 0, :rows], left[left_at, 1, :rows]
    right_high, right_low = right[right_at, 0, :, columns], right[right_at, 1, :, columns]
    return dot(high, right_high) + (dot(high, right_low) + dot(low, right_high))


def tiles(body):
    @pl.loop(0, WIDTH // TILE)
    def _(step):
        body(pl.ds(pl.multiple_of(step * TILE, TILE), TILE))


def kernel(
    inputs, in_weight, in_bias, out_weight, out_grad,
    outputs, grad_in, grad_w_in, grad_bias, grad_w_out,
    weights, left, turned, right, bias,
    local_sem, send_sem, recv_sem, *buffers,
):
    row, col = lax.axis_index("row"), lax.axis_index("col")
    zh, core = lax.div(row, 2), lax.rem(row, 2)
    zl, x, y = lax.div(col, 16), lax.rem(lax.div(col, 4), 4), lax.rem(col, 4)

    def device(dz=0, dc=0, dl=0, dx=0, dy=0):
        return (
            lax.rem(zh + dz, 4) * 2 + lax.rem(core + dc, 2),
            lax.rem(zl + dl, 2) * 16 + lax.rem(x + dx, 4) * 4 + lax.rem(y + dy, 4),
        )

    wide = (grad_w_out, grad_w_in)
    results = (outputs, grad_in)
    units = [tuple(buffers[8 * u : 8 * u + 8]) for u in range(len(UNITS))]
    count = [0, 0]
    sent = []
    waiting = {}

    def local(src, dst):
        copy = pltpu.make_async_copy(src, dst, local_sem.at[count[0]])
        count[0] += 1
        copy.start()
        return copy

    def inside(u):
        planes = UNITS[u][1]
        return None if len(planes) == 2 else zl == planes[0]

    def outside(u):
        planes = UNITS[u][1]
        return None if len(planes) == 2 else zl != planes[0]

    def place(u):
        return zl if len(UNITS[u][1]) == 2 else 0

    def when(condition, action):
        if condition is None:
            action()
        else:
            pl.when(condition)(action)

    def send(key, src, dst, to, only=None):
        copy = pltpu.make_async_remote_copy(
            src, dst, send_sem.at[count[1]], recv_sem.at[count[1]], device_id=to, device_id_type=MESH
        )
        count[1] += 1
        when(only, copy.start)
        waiting[key] = copy
        sent.append((copy, only))

    def arrived(*key, only=None):
        when(only, waiting[key].wait_recv)

    barrier = pltpu.get_barrier_semaphore()
    partners = [
        device(dz=1), device(dz=3), device(dc=1), device(dl=1),
        device(dx=1), device(dx=2), device(dx=3), device(dy=1), device(dy=2), device(dy=3),
    ]
    for partner in partners:
        pl.semaphore_signal(barrier, 1, device_id=partner, device_id_type=MESH)

    weight_copies = [local(in_weight, wide[0]), local(out_weight, wide[1])]
    bias_copy = local(in_bias, bias)
    own_copies = {}
    for u, (block, planes) in enumerate(UNITS):
        for a, source in enumerate((inputs, out_grad)):
            own = pltpu.make_async_copy(
                source.at[pl.ds(block * 8, 8)], units[u][0].at[a, y, x, place(u)], local_sem.at[count[0]]
            )
            count[0] += 1
            when(inside(u), own.start)
            own_copies[u, a] = own
    pl.semaphore_wait(barrier, len(partners))

    def shard(ref, lead, owner_core, owner):
        return ref.at[(*lead, owner_core * 2 + lax.div(owner, 2), pl.ds(lax.rem(owner, 2) * 2, 2))]

    def half(ref, lead, owner_core):
        return ref.at[(*lead, pl.ds(owner_core * 2, 2))]

    def part(ref, lead, owner):
        return ref.at[(*lead, lax.div(owner, 2), pl.ds(lax.rem(owner, 2) * 2, 2))]

    up, down = lax.rem(zh + 1, 4), lax.rem(zh + 3, 4)
    far = lax.rem(zh + 2, 4)

    def a0(u):
        gathered = units[u][0]
        for a, source in enumerate((inputs, out_grad)):
            rows = source.at[pl.ds(UNITS[u][0] * 8, 8)]
            send((u, "a0", a), rows, gathered.at[a, y, x, place(u)], device(dl=1), inside(u))

    def a1(u):
        gathered = units[u][0]
        for a in range(2):
            when(inside(u), own_copies[u, a].wait)
            arrived(u, "a0", a, only=outside(u))
            for o in range(1, 4):
                to = device(dx=o) if a == 0 else device(dy=o)
                block = gathered.at[a, y, x]
                send((u, "a1", a, o), block, block, to)

    def a2(u):
        gathered = units[u][0]
        for a in range(2):
            for o in range(1, 4):
                arrived(u, "a1", a, o)
            for o in range(1, 4):
                to = device(dy=o) if a == 0 else device(dx=o)
                block = gathered.at[0, y] if a == 0 else gathered.at[1, :, x]
                send((u, "a2", a, o), block, block, to)

    def prepare(which):
        weight_copies[which].wait()

        def body(columns):
            high, low = split(wide[which][:, columns])
            weights[which, 0, :, columns] = high
            weights[which, 1, :, columns] = low
            high, low = split(wide[which][:, columns].T)
            weights[2 + which, 0, columns, :] = high
            weights[2 + which, 1, columns, :] = low

        tiles(body)

    def flat(value):
        return value.reshape(-1, WIDTH)

    def project(u):
        gathered, partial, from_core = units[u][0], units[u][1], units[u][2]
        shape = partial.shape[1:-1]
        rows = shape[0] * shape[1] * shape[2] * shape[3]
        for a in range(2):
            for o in range(1, 4):
                arrived(u, "a2", a, o)
            high, low = split(flat(gathered[a]))
            left[a, 0, :rows] = high
            left[a, 1, :rows] = low

            def body(columns, a=a):
                value = dot3(left, a, rows, weights, 0 if a == 0 else 3, columns)
                partial[a, :, :, :, :, columns] = value.reshape(*shape, TILE)

            tiles(body)
            send((u, "b", a), half(partial, (a,), 1 - core), from_core.at[a], device(dc=1))

    def reduce_start(u):
        partial, from_core, ring = units[u][1], units[u][2], units[u][3]
        for a in range(2):
            arrived(u, "b", a)
            from_core[a] = from_core[a] + half(partial, (a,), core)[...]
        send((u, "c", 0), part(from_core, (0,), far), ring.at[0], device(dz=1))
        send((u, "c", 1), part(from_core, (1,), far), ring.at[1], device(dz=3))
        send((u, "c", 2), part(from_core, (1,), up), ring.at[2], device(dz=1))
        send((u, "c", 3), part(from_core, (0,), down), ring.at[3], device(dz=3))

    def reduce_relay(u):
        from_core, ring = units[u][2], units[u][3]
        arrived(u, "c", 0)
        ring[0] = ring[0] + part(from_core, (0,), up)[...]
        send((u, "d", 0), ring.at[0], ring.at[4], device(dz=1))
        arrived(u, "c", 1)
        ring[1] = ring[1] + part(from_core, (1,), down)[...]
        send((u, "d", 1), ring.at[1], ring.at[5], device(dz=3))

    def activate(u):
        from_core, ring, hidden = units[u][2], units[u][3], units[u][4]
        arrived(u, "c", 2)
        arrived(u, "c", 3)
        arrived(u, "d", 0)
        arrived(u, "d", 1)
        pre = flat(part(from_core, (0,), zh)[...] + (ring[3] + ring[4])) + bias[...].reshape(1, WIDTH)
        grad_act = flat(part(from_core, (1,), zh)[...] + (ring[2] + ring[5]))
        cdf = 0.5 * (1.0 + lax.erf(pre * inv_root_two))
        slopes = cdf + pre * jnp.exp(-0.5 * pre * pre) * inv_root_two_pi
        shape = ring.shape[1:]
        shard(hidden, (0,), core, zh)[...] = (pre * cdf).reshape(shape)
        shard(hidden, (1,), core, zh)[...] = (grad_act * slopes).reshape(shape)
        block = shard(hidden, (slice(None),), core, zh)
        send((u, "e", 0), block, block, device(dz=1))
        send((u, "e", 1), block, block, device(dz=3))
        send((u, "e", 2), block, block, device(dc=1))

    def gather_relay(u):
        hidden = units[u][4]
        arrived(u, "e", 0)
        block = shard(hidden, (0,), core, down)
        send((u, "f", 0), block, block, device(dz=1))
        arrived(u, "e", 1)
        block = shard(hidden, (1,), core, up)
        send((u, "f", 1), block, block, device(dz=3))
        block = shard(hidden, (slice(None),), core, down)
        send((u, "f", 2), block, block, device(dc=1))
        block = shard(hidden, (slice(None),), core, up)
        send((u, "f", 3), block, block, device(dc=1))

    def gather_last(u):
        hidden = units[u][4]
        for a in range(2):
            arrived(u, "f", a)
            block = shard(hidden, (a,), core, far)
            send((u, "g", a), block, block, device(dc=1))

    def expand(u):
        partial, hidden, first = units[u][1], units[u][4], units[u][5]
        shape = partial.shape[1:-1]
        rows = shape[0] * shape[1] * shape[2] * shape[3]
        arrived(u, "e", 2)
        arrived(u, "f", 2)
        arrived(u, "f", 3)
        arrived(u, "g", 0)
        arrived(u, "g", 1)
        for a in range(2):
            high, low = split(flat(hidden[a]))
            left[a, 0, :rows] = high
            left[a, 1, :rows] = low
            waiting[u, "b", a].wait_send()

            def body(columns, a=a):
                value = dot3(left, a, rows, weights, 1 if a == 0 else 2, columns)
                partial[a, :, :, :, :, columns] = value.reshape(*shape, TILE)

            tiles(body)
            for o in range(1, 4):
                if a == 0:
                    block, to = partial.at[0, lax.rem(y + o, 4)], device(dy=o)
                else:
                    block, to = partial.at[1, :, lax.rem(x + o, 4)], device(dx=o)
                send((u, "r", a, o), block, first.at[a, o - 1], to)

    def weight_grads(u):
        gathered, hidden = units[u][0], units[u][4]
        rows = gathered.shape[1] * gathered.shape[2] * gathered.shape[3] * gathered.shape[4]
        high, low = split(flat(hidden[0]).T)
        turned[0, 0, :, :rows] = high
        turned[0, 1, :, :rows] = low
        high, low = split(flat(gathered[0]).T)
        turned[1, 0, :, :rows] = high
        turned[1, 1, :, :rows] = low
        for a, value in enumerate((gathered[1], hidden[1])):
            high, low = split(flat(value))
            right[a, 0, :rows] = high
            right[a, 1, :rows] = low
        total = jnp.sum(flat(hidden[1]), axis=0)
        grad_bias[...] = total if u == 0 else grad_bias[...] + total

        def body(columns):
            for which in range(2):
                high, low = turned[which, 0, :, :rows], turned[which, 1, :, :rows]
                right_high, right_low = right[which, 0, :rows, columns], right[which, 1, :rows, columns]
                value = dot(high, right_high) + (dot(high, right_low) + dot(low, right_high))
                wide[which][:, columns] = value if u == 0 else wide[which][:, columns] + value

        tiles(body)

    def scatter_first(u):
        partial, first, second = units[u][1], units[u][5], units[u][6]
        for a in range(2):
            for o in range(1, 4):
                arrived(u, "r", a, o)
            own = partial[0, y] if a == 0 else partial[1, :, x]
            first[a, 0] = own + first[a, 0] + (first[a, 1] + first[a, 2])
            for o in range(1, 4):
                if a == 0:
                    block, to = first.at[0, 0, lax.rem(x + o, 4)], device(dx=o)
                else:
                    block, to = first.at[1, 0, lax.rem(y + o, 4)], device(dy=o)
                send((u, "s", a, o), block, second.at[a, o - 1], to)

    def scatter_second(u):
        first, second, third = units[u][5], units[u][6], units[u][7]
        for a in range(2):
            for o in range(1, 4):
                arrived(u, "s", a, o)
            own = first[0, 0, x] if a == 0 else first[1, 0, y]
            second[a, 0] = own + second[a, 0] + (second[a, 1] + second[a, 2])
            other = 1 - zl if len(UNITS[u][1]) == 2 else 0
            send((u, "t", a), second.at[a, 0, other], third.at[a], device(dl=1), outside(u))

    def scatter_last(u):
        second, third = units[u][6], units[u][7]
        rows = pl.ds(UNITS[u][0] * 8, 8)

        def add():
            for a in range(2):
                arrived(u, "t", a)
                results[a][rows] = second[a, 0, place(u)] + third[a]

        when(inside(u), add)

    stages = {
        "A0": a0, "A1": a1, "A2": a2, "W": prepare, "B": project, "C": reduce_start, "D": reduce_relay,
        "E": activate, "F": gather_relay, "G": gather_last, "M": expand, "N": weight_grads,
        "R": scatter_first, "S": scatter_second, "T": scatter_last,
    }
    for entry in SCHEDULE:
        name, u = entry.split()
        if name == "C" and u == "0":
            bias_copy.wait()
        stages[name](int(u))

    done = {id(waiting[u, "b", a]) for u in range(len(UNITS)) for a in range(2)}
    for copy, only in sent:
        if id(copy) not in done:
            when(only, copy.wait_send)


def hand_over(*refs):
    copies = [pltpu.make_async_copy(refs[i], refs[5 + i], refs[10].at[i]) for i in range(5)]
    for copy in copies:
        copy.start()
    for copy in copies:
        copy.wait()


def on_device(inputs, in_weight, in_bias, out_weight, out_grad):
    tokens = inputs.shape[0]
    buffers = []
    for _, planes in UNITS:
        n = len(planes)
        buffers += [
            pltpu.VMEM((2, 4, 4, n, 8, WIDTH), F32),
            pltpu.VMEM((2, 4, 4, n, 8, WIDTH), F32),
            pltpu.VMEM((2, 2, 4, n, 8, WIDTH), F32),
            pltpu.VMEM((6, 2, n, 8, WIDTH), F32),
            pltpu.VMEM((2, 4, 4, n, 8, WIDTH), F32),
            pltpu.VMEM((2, 3, 4, n, 8, WIDTH), F32),
            pltpu.VMEM((2, 3, n, 8, WIDTH), F32),
            pltpu.VMEM((2, 8, WIDTH), F32),
        ]
    copies = 45 * len(UNITS)
    anywhere = pl.BlockSpec(memory_space=pl.ANY)
    in_vmem = pl.BlockSpec(memory_space=pltpu.VMEM)
    in_hbm = pl.BlockSpec(memory_space=pltpu.HBM)
    shapes = [
        jax.ShapeDtypeStruct((tokens, WIDTH), F32),
        jax.ShapeDtypeStruct((tokens, WIDTH), F32),
        jax.ShapeDtypeStruct((WIDTH, WIDTH), F32),
        jax.ShapeDtypeStruct((WIDTH,), F32),
        jax.ShapeDtypeStruct((WIDTH, WIDTH), F32),
    ]
    made = pl.pallas_call(
        kernel,
        out_shape=[pltpu.VMEM(shape.shape, shape.dtype) for shape in shapes],
        in_specs=[anywhere] * 5,
        out_specs=[in_vmem] * 5,
        scratch_shapes=[
            pltpu.VMEM((4, 2, WIDTH, WIDTH), BF16),
            pltpu.VMEM((2, 2, 256, WIDTH), BF16),
            pltpu.VMEM((2, 2, WIDTH, 256), BF16),
            pltpu.VMEM((2, 2, 256, WIDTH), BF16),
            pltpu.VMEM((WIDTH,), F32),
            pltpu.SemaphoreType.DMA((8 + 2 * len(UNITS),)),
            pltpu.SemaphoreType.DMA((copies,)),
            pltpu.SemaphoreType.DMA((copies,)),
            *buffers,
        ],
        compiler_params=pltpu.CompilerParams(
            collective_id=0, has_side_effects=True, vmem_limit_bytes=52 * 2**20
        ),
        name="mlp",
    )(inputs, in_weight, in_bias, out_weight, out_grad)
    outputs, grad_in, grad_w_in, grad_bias, grad_w_out = pl.pallas_call(
        hand_over,
        out_shape=shapes,
        in_specs=[in_vmem] * 5,
        out_specs=[in_hbm] * 5,
        scratch_shapes=[pltpu.SemaphoreType.DMA((5,))],
        compiler_params=pltpu.CompilerParams(vmem_limit_bytes=2**20),
        name="hand_over",
    )(*[pltpu.with_memory_space_constraint(value, pltpu.VMEM) for value in made])
    return outputs, grad_in, grad_w_in, grad_bias, grad_w_out


def solution(mesh):
    in_specs = (P("col", "row"), P("row", "col"), P("col"), P("col", "row"), P("col", "row"))
    out_specs = (P("col", "row"), P("col", "row"), P("row", "col"), P("col"), P("col", "row"))
    return jax.shard_map(
        on_device, mesh=mesh, in_specs=in_specs, out_specs=out_specs, check_vma=False
    )
```

```python
import jax
import jax.numpy as jnp
from jax import lax
from jax.experimental import pallas as pl
from jax.experimental.pallas import tpu as pltpu
from jax.sharding import PartitionSpec as P

MESH = pl.DeviceIdType.MESH
F32 = jnp.float32
BF16 = jnp.bfloat16

inv_root_two = 0.7071067811865476
inv_root_two_pi = 0.3989422804014327

UNITS = ((0, (0,)), (0, (1,)), (1, (0, 1)), (2, (0, 1)), (3, (0,)), (3, (1,)))
SCHEDULE = (
    "Z1 0", "Z0 1", "Z1 4", "W0 0", "Z1 1", "Z0 2", "X0 1", "X1 0", "Z0 0", "X1 1", "X1 4", "Z0 3",
    "Z1 2", "Z0 5", "Z1 3", "X0 2", "Z1 5", "X0 0", "Y1 0", "Y0 1", "Y0 0", "Y1 1", "X1 2", "X1 5",
    "W1 0", "X0 5", "B0 1", "Z0 4", "C0 1", "B1 0", "X0 3", "X0 4", "C1 0", "Y0 2", "B0 0", "B1 1",
    "C0 0", "D0 1", "D1 0", "Y0 5", "Y1 2", "Y0 3", "D0 0", "Y0 4", "C1 1", "Y1 4", "E0 1", "Y1 5",
    "D1 1", "E0 0", "E1 0", "B0 2", "C0 2", "B1 2", "F0 0", "B1 4", "E1 1", "X1 3", "F1 0", "C1 4",
    "B0 3", "C1 2", "F0 1", "H0 0", "H0 1", "B0 4", "F1 1", "G1 0", "Y1 3", "D0 2", "C0 3", "G0 0",
    "G0 1", "M0 0", "H1 0", "C0 4", "G1 1", "D1 2", "H1 1", "M0 1", "E0 2", "D0 3", "M1 0", "E1 2",
    "D1 4", "B1 3", "H0 2", "C1 3", "M1 1", "B0 5", "F0 2", "F1 2", "N0 1", "D0 4", "D1 3", "B1 5",
    "G1 2", "R0 1", "E0 3", "N1 1", "H1 2", "C0 5", "G0 2", "E1 3", "M0 2", "F0 3", "H0 3", "E0 4",
    "E1 4", "M1 2", "N1 2", "F1 3", "C1 5", "G0 3", "N0 2", "M0 3", "D0 5", "G1 3", "H1 4", "H1 3",
    "F1 4", "R0 0", "R0 2", "R1 2", "F0 4", "R1 0", "S0 1", "D1 5", "M1 3", "H0 4", "E0 5", "N0 3",
    "E1 5", "G0 4", "M0 4", "S0 2", "H0 5", "G1 4", "N1 3", "R0 3", "F0 5", "G0 5", "M1 4", "M0 5",
    "R1 3", "F1 5", "H1 5", "G1 5", "M1 5", "N0 5", "R0 5", "S1 0", "R1 4", "R1 1", "S0 0", "S0 3",
    "R0 4", "S1 2", "T0 2", "T0 1", "S1 3", "R1 5", "S1 4", "S0 4", "S1 1", "T1 0", "T0 0", "T0 3",
    "S0 5", "S1 5", "T1 4", "N1 5", "T0 4", "T1 2", "T1 1", "T0 5", "T1 3", "T1 5",
)
WIDTH = 768
TILE = 256
LAG = 40
STRAIGHT = (5,)


def split(value):
    high = value.astype(BF16)
    return high, (value - high.astype(F32)).astype(BF16)


def dot(left, right):
    return lax.dot_general(left, right, (((1,), (0,)), ((), ())), preferred_element_type=F32)


def dot3(left, left_at, rows, right, right_at, columns):
    high, low = left[left_at, 0, :rows], left[left_at, 1, :rows]
    right_high, right_low = right[right_at, 0, :, columns], right[right_at, 1, :, columns]
    return dot(high, right_high) + (dot(high, right_low) + dot(low, right_high))


def tiles(body):
    @pl.loop(0, WIDTH // TILE)
    def _(step):
        body(pl.ds(pl.multiple_of(step * TILE, TILE), TILE))


def kernel(
    inputs, in_weight, in_bias, out_weight, out_grad,
    outputs, grad_in, grad_w_in, grad_bias, grad_w_out,
    weights, left, turned, right, bias,
    local_sem, send_sem, recv_sem, *buffers,
):
    row, col = lax.axis_index("row"), lax.axis_index("col")
    zh, core = lax.div(row, 2), lax.rem(row, 2)
    zl, x, y = lax.div(col, 16), lax.rem(lax.div(col, 4), 4), lax.rem(col, 4)

    def device(dz=0, dc=0, dl=0, dx=0, dy=0):
        return (
            lax.rem(zh + dz, 4) * 2 + lax.rem(core + dc, 2),
            lax.rem(zl + dl, 2) * 16 + lax.rem(x + dx, 4) * 4 + lax.rem(y + dy, 4),
        )

    wide = (grad_w_out, grad_w_in)
    results = (outputs, grad_in)
    units = [tuple(buffers[8 * u : 8 * u + 8]) for u in range(len(UNITS))]
    count = [0, 0]
    sent = []
    now = [0]
    waiting = {}

    def local(src, dst):
        copy = pltpu.make_async_copy(src, dst, local_sem.at[count[0]])
        count[0] += 1
        copy.start()
        return copy

    def inside(u):
        planes = UNITS[u][1]
        return None if len(planes) == 2 else zl == planes[0]

    def outside(u):
        planes = UNITS[u][1]
        return None if len(planes) == 2 else zl != planes[0]

    def place(u):
        return zl if len(UNITS[u][1]) == 2 else 0

    def when(condition, action):
        if condition is None:
            action()
        else:
            pl.when(condition)(action)

    def send(key, src, dst, to, only=None):
        copy = pltpu.make_async_remote_copy(
            src, dst, send_sem.at[count[1]], recv_sem.at[count[1]], device_id=to, device_id_type=MESH
        )
        count[1] += 1
        when(only, copy.start)
        waiting[key] = copy
        sent.append((now[0], key, copy, only))

    def settle(until):
        while sent and sent[0][0] <= until:
            _, key, copy, only = sent.pop(0)
            if key[1] != "b":
                when(only, copy.wait_send)

    def arrived(*key, only=None):
        when(only, waiting[key].wait_recv)

    barrier = pltpu.get_barrier_semaphore()
    partners = [
        device(dz=1), device(dz=2), device(dz=3), device(dc=1), device(dl=1),
        device(dx=1), device(dx=2), device(dx=3), device(dy=1), device(dy=2), device(dy=3),
    ]
    for partner in partners:
        pl.semaphore_signal(barrier, 1, device_id=partner, device_id_type=MESH)

    own_copies = {}
    for u, (block, planes) in enumerate(UNITS):
        for a, source in enumerate((inputs, out_grad)):
            own = pltpu.make_async_copy(
                source.at[pl.ds(block * 8, 8)], units[u][0].at[a, y, x, place(u)], local_sem.at[count[0]]
            )
            count[0] += 1
            when(inside(u), own.start)
            own_copies[u, a] = own
    weight_copies = [local(in_weight, wide[0]), local(out_weight, wide[1])]
    bias_copy = local(in_bias, bias)
    pl.semaphore_wait(barrier, len(partners))

    def shard(ref, lead, owner_core, owner):
        return ref.at[(*lead, owner_core * 2 + lax.div(owner, 2), pl.ds(lax.rem(owner, 2) * 2, 2))]

    def half(ref, lead, owner_core):
        return ref.at[(*lead, pl.ds(owner_core * 2, 2))]

    def part(ref, lead, owner):
        return ref.at[(*lead, lax.div(owner, 2), pl.ds(lax.rem(owner, 2) * 2, 2))]

    up, down = lax.rem(zh + 1, 4), lax.rem(zh + 3, 4)
    far = lax.rem(zh + 2, 4)

    onward, back = (device(dz=1), device(dz=3)), (device(dz=3), device(dz=1))
    ahead, behind = (up, down), (down, up)

    def exchange(u, a):
        rows = (inputs, out_grad)[a].at[pl.ds(UNITS[u][0] * 8, 8)]
        send((u, "z", a), rows, units[u][0].at[a, y, x, place(u)], device(dl=1), inside(u))

    def gather_first(u, a):
        when(inside(u), own_copies[u, a].wait)
        arrived(u, "z", a, only=outside(u))
        block = units[u][0].at[a, y, x]
        for o in (1, 3, 2):
            send((u, "x", a, o), block, block, device(dx=o) if a == 0 else device(dy=o))

    def gather_second(u, a):
        for o in (1, 2, 3):
            arrived(u, "x", a, o)
        block = units[u][0].at[0, y] if a == 0 else units[u][0].at[1, :, x]
        for o in (1, 3, 2):
            send((u, "y", a, o), block, block, device(dy=o) if a == 0 else device(dx=o))

    def prepare(which):
        weight_copies[which].wait()

        def body(columns):
            high, low = split(wide[which][:, columns])
            weights[which, 0, :, columns] = high
            weights[which, 1, :, columns] = low
            high, low = split(wide[which][:, columns].T)
            weights[2 + which, 0, columns, :] = high
            weights[2 + which, 1, columns, :] = low

        tiles(body)

    def flat(value):
        return value.reshape(-1, WIDTH)

    def project(u, a):
        gathered, partial, from_core = units[u][0], units[u][1], units[u][2]
        shape = partial.shape[1:-1]
        rows = shape[0] * shape[1] * shape[2] * shape[3]
        for o in range(1, 4):
            arrived(u, "y", a, o)
        high, low = split(flat(gathered[a]))
        left[a, 0, :rows] = high
        left[a, 1, :rows] = low

        def body(columns):
            value = dot3(left, a, rows, weights, 0 if a == 0 else 3, columns)
            partial[a, :, :, :, :, columns] = value.reshape(*shape, TILE)

        tiles(body)
        send((u, "b", a), half(partial, (a,), 1 - core), from_core.at[a], device(dc=1))

    def reduce_start(u, a):
        partial, from_core, ring = units[u][1], units[u][2], units[u][3]
        arrived(u, "b", a)
        from_core[a] = from_core[a] + half(partial, (a,), core)[...]
        send((u, "relay", a), part(from_core, (a,), far), ring.at[a], onward[a])
        send((u, "direct", a), part(from_core, (a,), behind[a]), ring.at[3 - a], back[a])

    def reduce_relay(u, a):
        from_core, ring = units[u][2], units[u][3]
        arrived(u, "relay", a)
        ring[a] = ring[a] + part(from_core, (a,), ahead[a])[...]
        send((u, "relayed", a), ring.at[a], ring.at[4 + a], onward[a])

    def activate(u, a):
        from_core, ring, hidden = units[u][2], units[u][3], units[u][4]
        arrived(u, "direct", a)
        arrived(u, "relayed", a)
        total = flat(part(from_core, (a,), zh)[...] + (ring[3 - a] + ring[4 + a]))
        shape = ring.shape[1:]
        if a == 0:
            if u == first_activated:
                bias_copy.wait()
            pre = total + bias[...].reshape(1, WIDTH)
            cdf = 0.5 * (1.0 + lax.erf(pre * inv_root_two))
            slopes = cdf + pre * jnp.exp(-0.5 * pre * pre) * inv_root_two_pi
            shard(hidden, (0,), core, zh)[...] = (pre * cdf).reshape(shape)
            ring[3] = slopes.reshape(shape)
        else:
            shard(hidden, (1,), core, zh)[...] = total.reshape(shape) * ring[3]
        block = shard(hidden, (a,), core, zh)
        send((u, "on", a), block, block, onward[a])
        send((u, "back", a), block, block, back[a])
        send((u, "own", a), block, block, device(dc=1))
        if u in STRAIGHT:
            send((u, "far", a), block, block, device(dz=2))

    def spread_relay(u, a):
        arrived(u, "on", a)
        block = shard(units[u][4], (a,), core, behind[a])
        if u not in STRAIGHT:
            send((u, "far", a), block, block, onward[a])
        send((u, "pass on", a), block, block, device(dc=1))

    def spread_back(u, a):
        arrived(u, "back", a)
        block = shard(units[u][4], (a,), core, ahead[a])
        send((u, "pass back", a), block, block, device(dc=1))

    def spread_far(u, a):
        arrived(u, "far", a)
        block = shard(units[u][4], (a,), core, far)
        send((u, "pass far", a), block, block, device(dc=1))

    def expand(u, a):
        partial, hidden, first = units[u][1], units[u][4], units[u][5]
        shape = partial.shape[1:-1]
        rows = shape[0] * shape[1] * shape[2] * shape[3]
        for name in ("own", "pass on", "pass back", "pass far"):
            arrived(u, name, a)
        high, low = split(flat(hidden[a]))
        left[a, 0, :rows] = high
        left[a, 1, :rows] = low
        waiting[u, "b", a].wait_send()

        def body(columns):
            value = dot3(left, a, rows, weights, 1 if a == 0 else 2, columns)
            partial[a, :, :, :, :, columns] = value.reshape(*shape, TILE)

        tiles(body)
        for o in (1, 3, 2):
            if a == 0:
                block, to = partial.at[0, lax.rem(y + o, 4)], device(dy=o)
            else:
                block, to = partial.at[1, :, lax.rem(x + o, 4)], device(dx=o)
            send((u, "r", a, o), block, first.at[a, o - 1], to)

    def weight_grads(u, a):
        group = [v for v in range(u + 1) if UNITS[v][0] == UNITS[u][0]]
        rows, total = 0, 0.0
        for v in group:
            gathered, hidden = units[v][0], units[v][4]
            lefts, rights = (hidden[0], gathered[1]) if a == 0 else (gathered[0], hidden[1])
            span = slice(rows, rows + gathered.shape[1] * gathered.shape[2] * gathered.shape[3] * gathered.shape[4])
            high, low = split(flat(lefts).T)
            turned[a, 0, :, span] = high
            turned[a, 1, :, span] = low
            high, low = split(flat(rights))
            right[a, 0, span] = high
            right[a, 1, span] = low
            rows = span.stop
            if a == 1:
                total = total + jnp.sum(flat(rights), axis=0)
        first = group[0] == 0
        if a == 1:
            grad_bias[...] = total if first else grad_bias[...] + total

        def body(columns):
            high, low = turned[a, 0, :, :rows], turned[a, 1, :, :rows]
            right_high, right_low = right[a, 0, :rows, columns], right[a, 1, :rows, columns]
            value = dot(high, right_high) + (dot(high, right_low) + dot(low, right_high))
            wide[a][:, columns] = value if first else wide[a][:, columns] + value

        tiles(body)

    def scatter_first(u, a):
        partial, first, second = units[u][1], units[u][5], units[u][6]
        for o in range(1, 4):
            arrived(u, "r", a, o)
        own = partial[0, y] if a == 0 else partial[1, :, x]
        first[a, 0] = own + first[a, 0] + (first[a, 1] + first[a, 2])
        for o in (1, 3, 2):
            if a == 0:
                block, to = first.at[0, 0, lax.rem(x + o, 4)], device(dx=o)
            else:
                block, to = first.at[1, 0, lax.rem(y + o, 4)], device(dy=o)
            send((u, "s", a, o), block, second.at[a, o - 1], to)

    def scatter_second(u, a):
        first, second, third = units[u][5], units[u][6], units[u][7]
        for o in range(1, 4):
            arrived(u, "s", a, o)
        own = first[0, 0, x] if a == 0 else first[1, 0, y]
        second[a, 0] = own + second[a, 0] + (second[a, 1] + second[a, 2])
        other = 1 - zl if len(UNITS[u][1]) == 2 else 0
        send((u, "t", a), second.at[a, 0, other], third.at[a], device(dl=1), outside(u))

    def scatter_last(u, a):
        second, third = units[u][6], units[u][7]

        def add():
            arrived(u, "t", a)
            results[a][pl.ds(UNITS[u][0] * 8, 8)] = second[a, 0, place(u)] + third[a]

        when(inside(u), add)

    stages = {
        "Z": exchange, "X": gather_first, "Y": gather_second, "B": project, "C": reduce_start,
        "D": reduce_relay, "E": activate, "F": spread_relay, "H": spread_back, "G": spread_far,
        "M": expand, "N": weight_grads, "R": scatter_first, "S": scatter_second, "T": scatter_last,
    }
    first_activated = int(next(entry for entry in SCHEDULE if entry[:2] == "E0").split()[1])
    for step, entry in enumerate(SCHEDULE):
        now[0] = step
        name, u = entry.split()
        if name[0] == "W":
            prepare(int(name[1]))
        else:
            stages[name[0]](int(u), int(name[1]))
        settle(step - LAG)
    settle(len(SCHEDULE))


def hand_over(*refs):
    copies = [pltpu.make_async_copy(refs[i], refs[5 + i], refs[10].at[i]) for i in range(5)]
    for copy in copies:
        copy.start()
    for copy in copies:
        copy.wait()


def on_device(inputs, in_weight, in_bias, out_weight, out_grad):
    tokens = inputs.shape[0]
    buffers = []
    for _, planes in UNITS:
        n = len(planes)
        buffers += [
            pltpu.VMEM((2, 4, 4, n, 8, WIDTH), F32),
            pltpu.VMEM((2, 4, 4, n, 8, WIDTH), F32),
            pltpu.VMEM((2, 2, 4, n, 8, WIDTH), F32),
            pltpu.VMEM((6, 2, n, 8, WIDTH), F32),
            pltpu.VMEM((2, 4, 4, n, 8, WIDTH), F32),
            pltpu.VMEM((2, 3, 4, n, 8, WIDTH), F32),
            pltpu.VMEM((2, 3, n, 8, WIDTH), F32),
            pltpu.VMEM((2, 8, WIDTH), F32),
        ]
    copies = 50 * len(UNITS)
    anywhere = pl.BlockSpec(memory_space=pl.ANY)
    in_vmem = pl.BlockSpec(memory_space=pltpu.VMEM)
    in_hbm = pl.BlockSpec(memory_space=pltpu.HBM)
    shapes = [
        jax.ShapeDtypeStruct((tokens, WIDTH), F32),
        jax.ShapeDtypeStruct((tokens, WIDTH), F32),
        jax.ShapeDtypeStruct((WIDTH, WIDTH), F32),
        jax.ShapeDtypeStruct((WIDTH,), F32),
        jax.ShapeDtypeStruct((WIDTH, WIDTH), F32),
    ]
    made = pl.pallas_call(
        kernel,
        out_shape=[pltpu.VMEM(shape.shape, shape.dtype) for shape in shapes],
        in_specs=[anywhere] * 5,
        out_specs=[in_vmem] * 5,
        scratch_shapes=[
            pltpu.VMEM((4, 2, WIDTH, WIDTH), BF16),
            pltpu.VMEM((2, 2, 256, WIDTH), BF16),
            pltpu.VMEM((2, 2, WIDTH, 256), BF16),
            pltpu.VMEM((2, 2, 256, WIDTH), BF16),
            pltpu.VMEM((WIDTH,), F32),
            pltpu.SemaphoreType.DMA((8 + 2 * len(UNITS),)),
            pltpu.SemaphoreType.DMA((copies,)),
            pltpu.SemaphoreType.DMA((copies,)),
            *buffers,
        ],
        compiler_params=pltpu.CompilerParams(
            collective_id=0, has_side_effects=True, vmem_limit_bytes=52 * 2**20
        ),
        name="mlp",
    )(inputs, in_weight, in_bias, out_weight, out_grad)
    outputs, grad_in, grad_w_in, grad_bias, grad_w_out = pl.pallas_call(
        hand_over,
        out_shape=shapes,
        in_specs=[in_vmem] * 5,
        out_specs=[in_hbm] * 5,
        scratch_shapes=[pltpu.SemaphoreType.DMA((5,))],
        compiler_params=pltpu.CompilerParams(vmem_limit_bytes=2**20),
        name="hand_over",
    )(*[pltpu.with_memory_space_constraint(value, pltpu.VMEM) for value in made])
    return outputs, grad_in, grad_w_in, grad_bias, grad_w_out


def solution(mesh):
    in_specs = (P("col", "row"), P("row", "col"), P("col"), P("col", "row"), P("col", "row"))
    out_specs = (P("col", "row"), P("col", "row"), P("row", "col"), P("col"), P("col", "row"))
    return jax.shard_map(
        on_device, mesh=mesh, in_specs=in_specs, out_specs=out_specs, check_vma=False
    )
```

```python
import jax
import jax.numpy as jnp
from jax import lax
from jax.experimental import pallas as pl
from jax.experimental.pallas import tpu as pltpu
from jax.sharding import PartitionSpec as P

MESH = pl.DeviceIdType.MESH
F32 = jnp.float32
BF16 = jnp.bfloat16

inv_root_two = 0.7071067811865476
inv_root_two_pi = 0.3989422804014327

UNITS = ((0, (0,)), (0, (1,)), (1, (0, 1)), (2, (0, 1)), (3, (0,)), (3, (1,)))
SCHEDULE = (
    "Z1 0", "Z0 1", "Z1 4", "W0 0", "Z1 1", "Z0 2", "X0 1", "X1 0", "Z0 0", "X1 1", "X1 4", "Z0 3",
    "Z1 2", "Z0 5", "Z1 3", "X0 2", "Z1 5", "X0 0", "Y1 0", "Y0 1", "Y0 0", "Y1 1", "X1 2", "X1 5",
    "W1 0", "X0 5", "B0 1", "Z0 4", "C0 1", "B1 0", "X0 3", "X0 4", "C1 0", "Y0 2", "B0 0", "B1 1",
    "C0 0", "D0 1", "D1 0", "Y0 5", "Y1 2", "Y0 3", "D0 0", "Y0 4", "C1 1", "Y1 4", "E0 1", "Y1 5",
    "D1 1", "E0 0", "E1 0", "B0 2", "C0 2", "B1 2", "F0 0", "B1 4", "E1 1", "X1 3", "F1 0", "C1 4",
    "B0 3", "C1 2", "F0 1", "H0 0", "H0 1", "B0 4", "F1 1", "G1 0", "Y1 3", "D0 2", "C0 3", "G0 0",
    "G0 1", "M0 0", "H1 0", "C0 4", "G1 1", "D1 2", "H1 1", "M0 1", "E0 2", "D0 3", "M1 0", "E1 2",
    "D1 4", "B1 3", "H0 2", "C1 3", "M1 1", "B0 5", "F0 2", "F1 2", "N0 1", "D0 4", "D1 3", "B1 5",
    "G1 2", "R0 1", "E0 3", "N1 1", "H1 2", "C0 5", "G0 2", "E1 3", "M0 2", "F0 3", "H0 3", "E0 4",
    "E1 4", "M1 2", "N1 2", "F1 3", "C1 5", "G0 3", "N0 2", "M0 3", "D0 5", "G1 3", "H1 4", "H1 3",
    "F1 4", "R0 0", "R0 2", "R1 2", "F0 4", "R1 0", "S0 1", "D1 5", "M1 3", "H0 4", "E0 5", "N0 3",
    "E1 5", "G0 4", "M0 4", "S0 2", "H0 5", "G1 4", "N1 3", "R0 3", "F0 5", "G0 5", "M1 4", "M0 5",
    "R1 3", "F1 5", "H1 5", "G1 5", "M1 5", "N0 5", "R0 5", "S1 0", "R1 4", "R1 1", "S0 0", "S0 3",
    "R0 4", "S1 2", "T0 2", "T0 1", "S1 3", "R1 5", "S1 4", "S0 4", "S1 1", "T1 0", "T0 0", "T0 3",
    "S0 5", "S1 5", "T1 4", "N1 5", "T0 4", "T1 2", "T1 1", "T0 5", "T1 3", "T1 5",
)
WIDTH = 768
TILE = 256
LAG = 40
STRAIGHT = (5,)


def split(value):
    high = value.astype(BF16)
    return high, (value - high.astype(F32)).astype(BF16)


def dot(left, right):
    return lax.dot_general(left, right, (((1,), (0,)), ((), ())), preferred_element_type=F32)


def dot3(left, left_at, rows, right, right_at, columns):
    high, low = left[left_at, 0, :rows], left[left_at, 1, :rows]
    right_high, right_low = right[right_at, 0, :, columns], right[right_at, 1, :, columns]
    return dot(high, right_high) + (dot(high, right_low) + dot(low, right_high))


def tiles(body):
    @pl.loop(0, WIDTH // TILE)
    def _(step):
        body(pl.ds(pl.multiple_of(step * TILE, TILE), TILE))


def kernel(
    inputs, in_weight, in_bias, out_weight, out_grad,
    outputs, grad_in, grad_w_in, grad_bias, grad_w_out,
    weights, left, turned, right, bias,
    local_sem, send_sem, recv_sem, *buffers,
):
    row, col = lax.axis_index("row"), lax.axis_index("col")
    zh, core = lax.div(row, 2), lax.rem(row, 2)
    zl, x, y = lax.div(col, 16), lax.rem(lax.div(col, 4), 4), lax.rem(col, 4)

    def device(dz=0, dc=0, dl=0, dx=0, dy=0):
        return (
            lax.rem(zh + dz, 4) * 2 + lax.rem(core + dc, 2),
            lax.rem(zl + dl, 2) * 16 + lax.rem(x + dx, 4) * 4 + lax.rem(y + dy, 4),
        )

    wide = (grad_w_out, grad_w_in)
    results = (outputs, grad_in)
    units = [tuple(buffers[8 * u : 8 * u + 8]) for u in range(len(UNITS))]
    count = [0, 0]
    sent = []
    now = [0]
    waiting = {}

    def local(src, dst):
        copy = pltpu.make_async_copy(src, dst, local_sem.at[count[0]])
        count[0] += 1
        copy.start()
        return copy

    def inside(u):
        planes = UNITS[u][1]
        return None if len(planes) == 2 else zl == planes[0]

    def outside(u):
        planes = UNITS[u][1]
        return None if len(planes) == 2 else zl != planes[0]

    def place(u):
        return zl if len(UNITS[u][1]) == 2 else 0

    def when(condition, action):
        if condition is None:
            action()
        else:
            pl.when(condition)(action)

    def send(key, src, dst, to, only=None):
        copy = pltpu.make_async_remote_copy(
            src, dst, send_sem.at[count[1]], recv_sem.at[count[1]], device_id=to, device_id_type=MESH
        )
        count[1] += 1
        when(only, copy.start)
        waiting[key] = copy
        sent.append((now[0], key, copy, only))

    def settle(until):
        while sent and sent[0][0] <= until:
            _, key, copy, only = sent.pop(0)
            if key[1] != "b":
                when(only, copy.wait_send)

    def arrived(*key, only=None):
        when(only, waiting[key].wait_recv)

    barrier = pltpu.get_barrier_semaphore()
    partners = [
        device(dz=1), device(dz=2), device(dz=3), device(dc=1), device(dl=1),
        device(dx=1), device(dx=2), device(dx=3), device(dy=1), device(dy=2), device(dy=3),
    ]
    for partner in partners:
        pl.semaphore_signal(barrier, 1, device_id=partner, device_id_type=MESH)

    own_copies = {}
    for u, (block, planes) in enumerate(UNITS):
        for a, source in enumerate((inputs, out_grad)):
            own = pltpu.make_async_copy(
                source.at[pl.ds(block * 8, 8)], units[u][0].at[a, y, x, place(u)], local_sem.at[count[0]]
            )
            count[0] += 1
            when(inside(u), own.start)
            own_copies[u, a] = own
    weight_copies = [local(in_weight, wide[0]), local(out_weight, wide[1])]
    bias_copy = local(in_bias, bias)
    pl.semaphore_wait(barrier, len(partners))

    def shard(ref, lead, owner_core, owner):
        return ref.at[(*lead, owner_core * 2 + lax.div(owner, 2), pl.ds(lax.rem(owner, 2) * 2, 2))]

    def half(ref, lead, owner_core):
        return ref.at[(*lead, pl.ds(owner_core * 2, 2))]

    def part(ref, lead, owner):
        return ref.at[(*lead, lax.div(owner, 2), pl.ds(lax.rem(owner, 2) * 2, 2))]

    up, down = lax.rem(zh + 1, 4), lax.rem(zh + 3, 4)
    far = lax.rem(zh + 2, 4)

    onward, back = (device(dz=1), device(dz=3)), (device(dz=3), device(dz=1))
    ahead, behind = (up, down), (down, up)

    def exchange(u, a):
        rows = (inputs, out_grad)[a].at[pl.ds(UNITS[u][0] * 8, 8)]
        send((u, "z", a), rows, units[u][0].at[a, y, x, place(u)], device(dl=1), inside(u))

    def gather_first(u, a):
        when(inside(u), own_copies[u, a].wait)
        arrived(u, "z", a, only=outside(u))
        block = units[u][0].at[a, y, x]
        for o in (2, 1, 3):
            send((u, "x", a, o), block, block, device(dx=o) if a == 0 else device(dy=o))

    def gather_second(u, a):
        for o in (1, 2, 3):
            arrived(u, "x", a, o)
        block = units[u][0].at[0, y] if a == 0 else units[u][0].at[1, :, x]
        for o in (2, 1, 3):
            send((u, "y", a, o), block, block, device(dy=o) if a == 0 else device(dx=o))

    def prepare(which):
        weight_copies[which].wait()

        def body(columns):
            high, low = split(wide[which][:, columns])
            weights[which, 0, :, columns] = high
            weights[which, 1, :, columns] = low
            high, low = split(wide[which][:, columns].T)
            weights[2 + which, 0, columns, :] = high
            weights[2 + which, 1, columns, :] = low

        tiles(body)

    def flat(value):
        return value.reshape(-1, WIDTH)

    def project(u, a):
        gathered, partial, from_core = units[u][0], units[u][1], units[u][2]
        shape = partial.shape[1:-1]
        rows = shape[0] * shape[1] * shape[2] * shape[3]
        for o in range(1, 4):
            arrived(u, "y", a, o)
        high, low = split(flat(gathered[a]))
        left[a, 0, :rows] = high
        left[a, 1, :rows] = low

        def body(columns):
            value = dot3(left, a, rows, weights, 0 if a == 0 else 3, columns)
            partial[a, :, :, :, :, columns] = value.reshape(*shape, TILE)

        tiles(body)
        send((u, "b", a), half(partial, (a,), 1 - core), from_core.at[a], device(dc=1))

    def reduce_start(u, a):
        partial, from_core, ring = units[u][1], units[u][2], units[u][3]
        arrived(u, "b", a)
        from_core[a] = from_core[a] + half(partial, (a,), core)[...]
        send((u, "relay", a), part(from_core, (a,), far), ring.at[a], onward[a])
        send((u, "direct", a), part(from_core, (a,), behind[a]), ring.at[3 - a], back[a])

    def reduce_relay(u, a):
        from_core, ring = units[u][2], units[u][3]
        arrived(u, "relay", a)
        ring[a] = ring[a] + part(from_core, (a,), ahead[a])[...]
        send((u, "relayed", a), ring.at[a], ring.at[4 + a], onward[a])

    def activate(u, a):
        from_core, ring, hidden = units[u][2], units[u][3], units[u][4]
        arrived(u, "direct", a)
        arrived(u, "relayed", a)
        total = flat(part(from_core, (a,), zh)[...] + (ring[3 - a] + ring[4 + a]))
        shape = ring.shape[1:]
        if a == 0:
            if u == first_activated:
                bias_copy.wait()
            pre = total + bias[...].reshape(1, WIDTH)
            cdf = 0.5 * (1.0 + lax.erf(pre * inv_root_two))
            slopes = cdf + pre * jnp.exp(-0.5 * pre * pre) * inv_root_two_pi
            shard(hidden, (0,), core, zh)[...] = (pre * cdf).reshape(shape)
            ring[3] = slopes.reshape(shape)
        else:
            shard(hidden, (1,), core, zh)[...] = total.reshape(shape) * ring[3]
        block = shard(hidden, (a,), core, zh)
        send((u, "on", a), block, block, onward[a])
        send((u, "back", a), block, block, back[a])
        send((u, "own", a), block, block, device(dc=1))
        if u in STRAIGHT:
            send((u, "far", a), block, block, device(dz=2))

    def spread_relay(u, a):
        arrived(u, "on", a)
        block = shard(units[u][4], (a,), core, behind[a])
        if u not in STRAIGHT:
            send((u, "far", a), block, block, onward[a])
        send((u, "pass on", a), block, block, device(dc=1))

    def spread_back(u, a):
        arrived(u, "back", a)
        block = shard(units[u][4], (a,), core, ahead[a])
        send((u, "pass back", a), block, block, device(dc=1))

    def spread_far(u, a):
        arrived(u, "far", a)
        block = shard(units[u][4], (a,), core, far)
        send((u, "pass far", a), block, block, device(dc=1))

    def expand(u, a):
        partial, hidden, first = units[u][1], units[u][4], units[u][5]
        shape = partial.shape[1:-1]
        rows = shape[0] * shape[1] * shape[2] * shape[3]
        for name in ("own", "pass on", "pass back", "pass far"):
            arrived(u, name, a)
        high, low = split(flat(hidden[a]))
        left[a, 0, :rows] = high
        left[a, 1, :rows] = low
        waiting[u, "b", a].wait_send()

        def body(columns):
            value = dot3(left, a, rows, weights, 1 if a == 0 else 2, columns)
            partial[a, :, :, :, :, columns] = value.reshape(*shape, TILE)

        tiles(body)
        for o in (2, 1, 3):
            if a == 0:
                block, to = partial.at[0, lax.rem(y + o, 4)], device(dy=o)
            else:
                block, to = partial.at[1, :, lax.rem(x + o, 4)], device(dx=o)
            send((u, "r", a, o), block, first.at[a, o - 1], to)

    def weight_grads(u, a):
        group = [v for v in range(u + 1) if UNITS[v][0] == UNITS[u][0]]
        rows, total = 0, 0.0
        for v in group:
            gathered, hidden = units[v][0], units[v][4]
            lefts, rights = (hidden[0], gathered[1]) if a == 0 else (gathered[0], hidden[1])
            span = slice(rows, rows + gathered.shape[1] * gathered.shape[2] * gathered.shape[3] * gathered.shape[4])
            high, low = split(flat(lefts).T)
            turned[a, 0, :, span] = high
            turned[a, 1, :, span] = low
            high, low = split(flat(rights))
            right[a, 0, span] = high
            right[a, 1, span] = low
            rows = span.stop
            if a == 1:
                total = total + jnp.sum(flat(rights), axis=0)
        first = group[0] == 0
        if a == 1:
            grad_bias[...] = total if first else grad_bias[...] + total

        def body(columns):
            high, low = turned[a, 0, :, :rows], turned[a, 1, :, :rows]
            right_high, right_low = right[a, 0, :rows, columns], right[a, 1, :rows, columns]
            value = dot(high, right_high) + (dot(high, right_low) + dot(low, right_high))
            wide[a][:, columns] = value if first else wide[a][:, columns] + value

        tiles(body)

    def scatter_first(u, a):
        partial, first, second = units[u][1], units[u][5], units[u][6]
        for o in range(1, 4):
            arrived(u, "r", a, o)
        own = partial[0, y] if a == 0 else partial[1, :, x]
        first[a, 0] = own + first[a, 0] + (first[a, 1] + first[a, 2])
        for o in (2, 1, 3):
            if a == 0:
                block, to = first.at[0, 0, lax.rem(x + o, 4)], device(dx=o)
            else:
                block, to = first.at[1, 0, lax.rem(y + o, 4)], device(dy=o)
            send((u, "s", a, o), block, second.at[a, o - 1], to)

    def scatter_second(u, a):
        first, second, third = units[u][5], units[u][6], units[u][7]
        for o in range(1, 4):
            arrived(u, "s", a, o)
        own = first[0, 0, x] if a == 0 else first[1, 0, y]
        second[a, 0] = own + second[a, 0] + (second[a, 1] + second[a, 2])
        other = 1 - zl if len(UNITS[u][1]) == 2 else 0
        send((u, "t", a), second.at[a, 0, other], third.at[a], device(dl=1), outside(u))

    def scatter_last(u, a):
        second, third = units[u][6], units[u][7]

        def add():
            arrived(u, "t", a)
            results[a][pl.ds(UNITS[u][0] * 8, 8)] = second[a, 0, place(u)] + third[a]

        when(inside(u), add)

    stages = {
        "Z": exchange, "X": gather_first, "Y": gather_second, "B": project, "C": reduce_start,
        "D": reduce_relay, "E": activate, "F": spread_relay, "H": spread_back, "G": spread_far,
        "M": expand, "N": weight_grads, "R": scatter_first, "S": scatter_second, "T": scatter_last,
    }
    first_activated = int(next(entry for entry in SCHEDULE if entry[:2] == "E0").split()[1])
    for step, entry in enumerate(SCHEDULE):
        now[0] = step
        name, u = entry.split()
        if name[0] == "W":
            prepare(int(name[1]))
        else:
            stages[name[0]](int(u), int(name[1]))
        settle(step - LAG)
    settle(len(SCHEDULE))


def hand_over(*refs):
    copies = [pltpu.make_async_copy(refs[i], refs[5 + i], refs[10].at[i]) for i in range(5)]
    for copy in copies:
        copy.start()
    for copy in copies:
        copy.wait()


def on_device(inputs, in_weight, in_bias, out_weight, out_grad):
    tokens = inputs.shape[0]
    buffers = []
    for _, planes in UNITS:
        n = len(planes)
        buffers += [
            pltpu.VMEM((2, 4, 4, n, 8, WIDTH), F32),
            pltpu.VMEM((2, 4, 4, n, 8, WIDTH), F32),
            pltpu.VMEM((2, 2, 4, n, 8, WIDTH), F32),
            pltpu.VMEM((6, 2, n, 8, WIDTH), F32),
            pltpu.VMEM((2, 4, 4, n, 8, WIDTH), F32),
            pltpu.VMEM((2, 3, 4, n, 8, WIDTH), F32),
            pltpu.VMEM((2, 3, n, 8, WIDTH), F32),
            pltpu.VMEM((2, 8, WIDTH), F32),
        ]
    copies = 50 * len(UNITS)
    anywhere = pl.BlockSpec(memory_space=pl.ANY)
    in_vmem = pl.BlockSpec(memory_space=pltpu.VMEM)
    in_hbm = pl.BlockSpec(memory_space=pltpu.HBM)
    shapes = [
        jax.ShapeDtypeStruct((tokens, WIDTH), F32),
        jax.ShapeDtypeStruct((tokens, WIDTH), F32),
        jax.ShapeDtypeStruct((WIDTH, WIDTH), F32),
        jax.ShapeDtypeStruct((WIDTH,), F32),
        jax.ShapeDtypeStruct((WIDTH, WIDTH), F32),
    ]
    made = pl.pallas_call(
        kernel,
        out_shape=[pltpu.VMEM(shape.shape, shape.dtype) for shape in shapes],
        in_specs=[anywhere] * 5,
        out_specs=[in_vmem] * 5,
        scratch_shapes=[
            pltpu.VMEM((4, 2, WIDTH, WIDTH), BF16),
            pltpu.VMEM((2, 2, 256, WIDTH), BF16),
            pltpu.VMEM((2, 2, WIDTH, 256), BF16),
            pltpu.VMEM((2, 2, 256, WIDTH), BF16),
            pltpu.VMEM((WIDTH,), F32),
            pltpu.SemaphoreType.DMA((8 + 2 * len(UNITS),)),
            pltpu.SemaphoreType.DMA((copies,)),
            pltpu.SemaphoreType.DMA((copies,)),
            *buffers,
        ],
        compiler_params=pltpu.CompilerParams(
            collective_id=0, has_side_effects=True, vmem_limit_bytes=52 * 2**20
        ),
        name="mlp",
    )(inputs, in_weight, in_bias, out_weight, out_grad)
    outputs, grad_in, grad_w_in, grad_bias, grad_w_out = pl.pallas_call(
        hand_over,
        out_shape=shapes,
        in_specs=[in_vmem] * 5,
        out_specs=[in_hbm] * 5,
        scratch_shapes=[pltpu.SemaphoreType.DMA((5,))],
        compiler_params=pltpu.CompilerParams(vmem_limit_bytes=2**20),
        name="hand_over",
    )(*[pltpu.with_memory_space_constraint(value, pltpu.VMEM) for value in made])
    return outputs, grad_in, grad_w_in, grad_bias, grad_w_out


def solution(mesh):
    in_specs = (P("col", "row"), P("row", "col"), P("col"), P("col", "row"), P("col", "row"))
    out_specs = (P("col", "row"), P("col", "row"), P("row", "col"), P("col"), P("col", "row"))
    return jax.shard_map(
        on_device, mesh=mesh, in_specs=in_specs, out_specs=out_specs, check_vma=False
    )
```
